512 devices in a mesh: prow: 16 (over z), pcol: 32 (over x, y, core).
Axes of the slice: x: 4, y: 4, z: 16, core: 2. Of those that a mesh axis runs over, the one named last changes fastest.
Arguments:
- matrix: float32 [8192, 8192], P('prow', 'pcol'), may hold values from -6 to 6
- factored_panel: float32 [8192, 256], P('prow', 'pcol')
- pivots: int32 [256], replicated, may hold values from 0 to 8191, as said below
Outputs:
- updated: float32 [8192, 8192], P('prow', 'pcol')
The draws below stay inside these ranges and needn't reach their ends.
Inputs may be any that keep to these rules, and one draw needn't show every extreme that they name: pivots[j] is j or larger for every j; 8191 appears among the entries.
All inputs are finite; a program needn't handle non-finite values.
Results may differ from the reference program's by a relative error of at most 0.000055.
Values sent between devices are 32-bit elements; how exact they have to be, the bound alone decides.
No kernel may reach another device: no remote copies, remote signals or barrier semaphores. Data moves between devices by JAX's collectives and lax.ppermute only.
A program may use at most 64 MiB of HBM per device.

```python
import math
from functools import partial
import jax
import jax.numpy as jnp
from jax import lax

NB = 256
N = 8192


def draw_factored_panel(key, part):
    key = jax.random.fold_in(key, 2)
    values = jax.random.normal(key, (N, NB), jnp.float32)
    row_ids = jnp.arange(N, dtype=jnp.int32)[:, None]
    col_ids = jnp.arange(NB, dtype=jnp.int32)[None, :]
    top_part = jnp.where(col_ids < row_ids, values * (0.5 / math.sqrt(NB)), 0.0)
    low_part = values * (1.0 / math.sqrt(NB))
    return jnp.where(row_ids < NB, top_part, low_part).astype(jnp.float32)


def draw_pivots(key, part):
    key = jax.random.fold_in(key, 5)
    key_a, key_b = jax.random.split(key)
    column = jnp.arange(NB, dtype=jnp.int32)
    raw_bits = jax.random.randint(key_a, (NB,), 0, 1073741824, dtype=jnp.int32)
    chosen = column + raw_bits % (N - column)
    forced = jax.random.randint(key_b, (), 0, NB, dtype=jnp.int32)
    return jnp.where(column == forced, N - 1, chosen).astype(jnp.int32)


def block_scale(own_key, extent, cuts, least, top_value):
    def one(position, shards_of):
        draws = jax.random.uniform(jax.random.fold_in(jax.random.fold_in(own_key, 6), position), (shards_of,), jnp.float32, least / len(cuts), top_value / len(cuts))
        return jnp.repeat(jnp.exp(draws), extent[position] // shards_of).reshape((-1,) + (1,) * (len(extent) - position - 1))

    gain = one(*cuts[0])
    for cut in cuts[1:]:
        gain = gain * one(*cut)
    return gain


def noise(own_key, dims, deviation, most, pieces=(), held_as=jnp.bfloat16):
    gain = block_scale(own_key, dims, pieces, -0.22, 0.18) if pieces else 1.0
    drawn = jax.random.normal(own_key, dims, jnp.float32) * deviation * gain
    return jnp.minimum(jnp.maximum(drawn, -most), most).astype(held_as)


def setup_inputs(seed: int = 0) -> dict:
    key_of = jax.random.split(jax.random.key(seed), 4)
    return {
        "matrix": noise(key_of[0], (N, N), 1.0, 6.0, ((0, 16), (1, 32)), jnp.float32),
        "factored_panel": draw_factored_panel(jax.random.fold_in(key_of[3], 71), 0),
        "pivots": draw_pivots(jax.random.fold_in(key_of[3], 71), 0),
    }


def exchange_rows(pivots, column, row_order):
    target = pivots[column]
    first = row_order[column]
    second = row_order[target]
    return row_order.at[column].set(second).at[target].set(first)

def reference(matrix, factored_panel, pivots):
    all_rows = matrix.shape[0]
    row_order = lax.fori_loop(0, NB, partial(exchange_rows, pivots), jnp.arange(all_rows, dtype=jnp.int32))
    swapped = jnp.take(matrix, row_order, axis=0)
    lower_tri = jnp.tril(factored_panel[:NB], -1) + jnp.eye(NB, dtype=jnp.float32)
    upper_rows = jax.scipy.linalg.solve_triangular(lower_tri, swapped[:NB], lower=True, unit_diagonal=True)
    below = swapped[NB:] - jnp.dot(factored_panel[NB:].astype(jnp.float32), upper_rows.astype(jnp.float32), precision=lax.Precision.HIGHEST, preferred_element_type=jnp.float32)
    return jnp.concatenate([upper_rows, below], axis=0)
```

```python
import jax
import jax.numpy as jnp
from jax import lax
from jax.experimental import pallas as pl
from jax.experimental.pallas import tpu as pltpu
from jax.sharding import PartitionSpec as P

HIGHEST = lax.Precision.HIGHEST
VMEM = pl.BlockSpec(memory_space=pltpu.VMEM)
SMEM = pl.BlockSpec(memory_space=pltpu.SMEM)


def dot_lhs_t(a, b):
    return lax.dot_general(
        a, b, (((0,), (0,)), ((), ())), precision=HIGHEST, preferred_element_type=jnp.float32
    )


def dot(a, b):
    return jnp.dot(a, b, precision=HIGHEST, preferred_element_type=jnp.float32)


def pack_kernel(pivots_ref, matrix_ref, panel_ref, send_ref, table_ref, order_ref):
    nb = pivots_ref.shape[0]
    rows = matrix_ref.shape[0]
    slots = nb // send_ref.shape[0]
    me = lax.axis_index("prow")

    def start(j, _):
        target = pivots_ref[j]
        order_ref[target] = target
        order_ref[j] = j
        return 0

    lax.fori_loop(0, nb, start, 0, unroll=8)

    def exchange(j, _):
        target = pivots_ref[j]
        first = order_ref[j]
        second = order_ref[target]
        order_ref[j] = second
        order_ref[target] = first
        return 0

    lax.fori_loop(0, nb, exchange, 0, unroll=8)

    def place(i, count):
        row = order_ref[i]
        partner = order_ref[row]
        table_ref[i] = row
        table_ref[nb + i] = partner
        mine = row - me * rows
        owned = (mine >= 0) & (mine < rows)
        table_ref[2 * nb + count] = i
        take = jnp.where(owned, mine, jnp.where(me == 0, partner, 0))
        send_ref[i // slots, pl.ds(i % slots, 1), :] = matrix_ref[pl.ds(take, 1), :]
        return count + jnp.where(owned & (row >= nb), 1, 0)

    count = lax.fori_loop(0, nb, place, 0, unroll=8)
    table_ref[3 * nb] = count
    lower_piece = panel_ref[:, :nb]
    for d in range(send_ref.shape[0]):
        send_ref[d, slots:, :] = lower_piece


def sort_kernel(table_ref, arrived_ref, panel_ref, send_ref, pieces_ref):
    planes = arrived_ref.shape[0]
    rows = panel_ref.shape[1]
    slots = send_ref.shape[1] // 2
    me = lax.axis_index("prow")
    for k in range(slots):
        owner = table_ref[me * slots + k] // rows
        send_ref[0, k : k + 1, :] = arrived_ref[owner, k : k + 1, :]
    send_ref[0, slots:, :] = arrived_ref[0, :slots, :]
    both = send_ref[0]
    for d in range(1, planes):
        send_ref[d] = both
    pieces_ref[:, :rows] = panel_ref[...]
    pieces_ref[:, rows:] = arrived_ref[0, slots:, :]


def invert_upper(block):
    size = block.shape[0]
    row = lax.broadcasted_iota(jnp.int32, (size, size), 0)
    col = lax.broadcasted_iota(jnp.int32, (size, size), 1)
    inverse = None
    width = 1
    while width < size:
        pair = ((row ^ col) & ~(2 * width - 1)) == 0
        cross = jnp.where(pair & ((row & width) == 0) & ((col & width) != 0), block, 0.0)
        if inverse is None:
            inverse = jnp.where(row == col, 1.0, 0.0) - cross
        else:
            inverse = inverse - dot(dot(inverse, cross), inverse)
        width *= 2
    return inverse


def update_kernel(table_ref, gathered_ref, arrived_ref, matrix_ref, out_ref, upper_ref):
    nb = upper_ref.shape[0]
    rows = matrix_ref.shape[0]
    planes = arrived_ref.shape[0]
    slots = nb // planes
    half = nb // 2
    me = lax.axis_index("prow")
    first = invert_upper(gathered_ref[:half, rows : rows + half])
    second = invert_upper(gathered_ref[half:, rows + half :])
    for d in range(planes):
        upper_ref[d * slots : (d + 1) * slots, :] = arrived_ref[d, :slots, :]
    top = dot_lhs_t(first, upper_ref[:half])
    rest = upper_ref[half:] - dot_lhs_t(gathered_ref[:half, rows + half :], top)
    upper_ref[:half] = top
    upper_ref[half:] = dot_lhs_t(second, rest)
    out_ref[...] = matrix_ref[...]

    def patch(n, _):
        slot = table_ref[2 * nb + n]
        target = table_ref[slot] - me * rows
        far = arrived_ref[slot // slots, pl.ds(slots + slot % slots, 1), :]
        near = matrix_ref[pl.ds(jnp.where(me == 0, table_ref[nb + slot], 0), 1), :]
        out_ref[pl.ds(target, 1), :] = jnp.where(me == 0, near, far)
        return 0

    lax.fori_loop(0, table_ref[3 * nb], patch, 0)
    out_ref[...] -= dot_lhs_t(gathered_ref[:, :rows], upper_ref[...])

    @pl.when(me == 0)
    def _():
        out_ref[:nb, :] = upper_ref[...]


def call(kernel, outs, in_specs, out_specs, scratch=()):
    return pl.pallas_call(
        kernel,
        out_shape=outs,
        in_specs=in_specs,
        out_specs=out_specs,
        scratch_shapes=list(scratch),
        compiler_params=pltpu.CompilerParams(vmem_limit_bytes=16 * 1024 * 1024),
    )


def local(matrix, factored_panel, pivots):
    rows, cols = matrix.shape
    nb = pivots.shape[0]
    planes = lax.axis_size("prow")
    slots = nb // planes
    width = factored_panel.shape[1]
    f32 = jnp.float32
    panel = factored_panel.T
    send, table = call(
        pack_kernel,
        (
            jax.ShapeDtypeStruct((planes, slots + width, cols), f32),
            jax.ShapeDtypeStruct((4 * nb,), jnp.int32),
        ),
        [SMEM, VMEM, VMEM],
        (VMEM, SMEM),
        [pltpu.SMEM((rows * planes,), jnp.int32)],
    )(pivots, matrix, panel)
    arrived = lax.all_to_all(send, "prow", 0, 0)
    send, pieces = call(
        sort_kernel,
        (
            jax.ShapeDtypeStruct((planes, 2 * slots, cols), f32),
            jax.ShapeDtypeStruct((width, rows + nb), f32),
        ),
        [SMEM, VMEM, VMEM],
        (VMEM, VMEM),
    )(table, arrived, panel)
    gathered = lax.all_gather(pieces, "pcol", axis=0, tiled=True)
    arrived = lax.all_to_all(send, "prow", 0, 0)
    return call(
        update_kernel,
        jax.ShapeDtypeStruct((rows, cols), f32),
        [SMEM, VMEM, VMEM, VMEM],
        VMEM,
        [pltpu.VMEM((nb, cols), f32)],
    )(table, gathered, arrived, matrix)


def solution(mesh):
    return jax.shard_map(
        local,
        mesh=mesh,
        in_specs=(P("prow", "pcol"), P("prow", "pcol"), P()),
        out_specs=P("prow", "pcol"),
        check_vma=False,
    )
```

```python
import jax
import jax.numpy as jnp
from jax import lax
from jax.experimental import pallas as pl
from jax.experimental.pallas import tpu as pltpu
from jax.sharding import PartitionSpec as P

HIGHEST = lax.Precision.HIGHEST
VMEM = pl.BlockSpec(memory_space=pltpu.VMEM)
HBM = pl.BlockSpec(memory_space=pltpu.HBM)
SMEM = pl.BlockSpec(memory_space=pltpu.SMEM)


def dot_lhs_t(a, b):
    return lax.dot_general(
        a, b, (((0,), (0,)), ((), ())), precision=HIGHEST, preferred_element_type=jnp.float32
    )


def dot(a, b):
    return jnp.dot(a, b, precision=HIGHEST, preferred_element_type=jnp.float32)


def pack_kernel(pivots_ref, matrix_hbm, panel_hbm, send_ref, table_ref, order_ref, matrix_ref, panel_ref, sem):
    nb = pivots_ref.shape[0]
    rows = matrix_ref.shape[0]
    planes = send_ref.shape[0]
    slots = nb // planes
    me = lax.axis_index("prow")
    fetch_matrix = pltpu.make_async_copy(matrix_hbm, matrix_ref, sem.at[0])
    fetch_panel = pltpu.make_async_copy(panel_hbm, panel_ref, sem.at[1])
    fetch_matrix.start()
    fetch_panel.start()

    def start(j, _):
        target = pivots_ref[j]
        order_ref[target] = target
        order_ref[j] = j
        return 0

    lax.fori_loop(0, nb, start, 0, unroll=16)

    def exchange(j, _):
        target = pivots_ref[j]
        first = order_ref[j]
        second = order_ref[target]
        order_ref[j] = second
        order_ref[target] = first
        return 0

    lax.fori_loop(0, nb, exchange, 0, unroll=16)
    fetch_panel.wait()
    lower_piece = panel_ref[:, :nb]
    for d in range(planes):
        send_ref[d, slots:, :] = lower_piece
    fetch_matrix.wait()
    base = me * rows

    def place(d, count):
        for k in range(slots):
            i = d * slots + k
            row = order_ref[i]
            partner = order_ref[row]
            mine = row - base
            owned = (mine >= 0) & (mine < rows)
            table_ref[i] = row
            table_ref[nb + count] = i
            table_ref[2 * nb + count] = mine
            table_ref[3 * nb + count] = partner
            take = jnp.where(owned, mine, jnp.where(me == 0, partner, 0))
            send_ref[d, k : k + 1, :] = matrix_ref[pl.ds(take, 1), :]
            count = count + jnp.where(owned & (row >= nb), 1, 0)
        return count

    table_ref[4 * nb] = lax.fori_loop(0, planes, place, 0)


def sort_kernel(table_ref, arrived_ref, panel_ref, send_ref, pieces_ref):
    planes = arrived_ref.shape[0]
    rows = panel_ref.shape[1]
    slots = send_ref.shape[1] // 2
    me = lax.axis_index("prow")
    pieces_ref[:, :rows] = panel_ref[...]
    pieces_ref[:, rows:] = arrived_ref[0, slots:, :]
    for k in range(slots):
        owner = table_ref[me * slots + k] // rows
        send_ref[0, k : k + 1, :] = arrived_ref[owner, k : k + 1, :]
    send_ref[0, slots:, :] = arrived_ref[0, :slots, :]
    both = send_ref[0]
    for d in range(1, planes):
        send_ref[d] = both


def invert_upper(block):
    size = block.shape[0]
    row = lax.broadcasted_iota(jnp.int32, (size, size), 0)
    col = lax.broadcasted_iota(jnp.int32, (size, size), 1)
    inverse = None
    width = 1
    while width < size:
        pair = ((row ^ col) & ~(2 * width - 1)) == 0
        cross = jnp.where(pair & ((row & width) == 0) & ((col & width) != 0), block, 0.0)
        if inverse is None:
            inverse = jnp.where(row == col, 1.0, 0.0) - cross
        else:
            inverse = inverse - dot(dot(inverse, cross), inverse)
        width *= 2
    return inverse


def invert_kernel(gathered_ref, inverse_ref):
    half = inverse_ref.shape[0] // 2
    rows = gathered_ref.shape[1] - 2 * half
    inverse_ref[:half] = invert_upper(gathered_ref[:half, rows : rows + half])
    inverse_ref[half:] = invert_upper(gathered_ref[half:, rows + half :])


def update_kernel(table_ref, gathered_ref, inverse_ref, arrived_ref, matrix_ref, out_ref, upper_ref):
    nb = upper_ref.shape[0]
    rows = matrix_ref.shape[0]
    planes = arrived_ref.shape[0]
    slots = nb // planes
    half = nb // 2
    me = lax.axis_index("prow")
    for d in range(planes):
        upper_ref[d * slots : (d + 1) * slots, :] = arrived_ref[d, :slots, :]
    top = dot_lhs_t(inverse_ref[:half], upper_ref[:half])
    rest = upper_ref[half:] - dot_lhs_t(gathered_ref[:half, rows + half :], top)
    upper_ref[:half] = top
    upper_ref[half:] = dot_lhs_t(inverse_ref[half:], rest)
    out_ref[...] = matrix_ref[...]

    def patch(n, _):
        slot = table_ref[nb + n]
        far = arrived_ref[slot // slots, pl.ds(slots + slot % slots, 1), :]
        near = matrix_ref[pl.ds(jnp.where(me == 0, table_ref[3 * nb + n], 0), 1), :]
        out_ref[pl.ds(table_ref[2 * nb + n], 1), :] = jnp.where(me == 0, near, far)
        return 0

    lax.fori_loop(0, table_ref[4 * nb], patch, 0)
    out_ref[...] -= dot_lhs_t(gathered_ref[:, :rows], upper_ref[...])

    @pl.when(me == 0)
    def _():
        out_ref[:nb, :] = upper_ref[...]


def call(kernel, outs, in_specs, out_specs, scratch=()):
    return pl.pallas_call(
        kernel,
        out_shape=outs,
        in_specs=in_specs,
        out_specs=out_specs,
        scratch_shapes=list(scratch),
        compiler_params=pltpu.CompilerParams(vmem_limit_bytes=16 * 1024 * 1024),
    )


def local(matrix, factored_panel, pivots):
    rows, cols = matrix.shape
    nb = pivots.shape[0]
    planes = lax.axis_size("prow")
    slots = nb // planes
    width = factored_panel.shape[1]
    f32 = jnp.float32
    panel = factored_panel.T
    send, table = call(
        pack_kernel,
        (
            jax.ShapeDtypeStruct((planes, slots + width, cols), f32),
            jax.ShapeDtypeStruct((8 * nb,), jnp.int32),
        ),
        [SMEM, HBM, HBM],
        (VMEM, SMEM),
        [
            pltpu.SMEM((rows * planes,), jnp.int32),
            pltpu.VMEM((rows, cols), f32),
            pltpu.VMEM((width, rows), f32),
            pltpu.SemaphoreType.DMA((2,)),
        ],
    )(pivots, matrix, panel)
    arrived = lax.all_to_all(send, "prow", 0, 0)
    send, pieces = call(
        sort_kernel,
        (
            jax.ShapeDtypeStruct((planes, 2 * slots, cols), f32),
            jax.ShapeDtypeStruct((width, rows + nb), f32),
        ),
        [SMEM, VMEM, VMEM],
        (VMEM, VMEM),
    )(table, arrived, panel)
    gathered = lax.all_gather(pieces, "pcol", axis=0, tiled=True)
    arrived = lax.all_to_all(send, "prow", 0, 0)
    inverse = call(invert_kernel, jax.ShapeDtypeStruct((nb, nb // 2), f32), [VMEM], VMEM)(gathered)
    return call(
        update_kernel,
        jax.ShapeDtypeStruct((rows, cols), f32),
        [SMEM, VMEM, VMEM, VMEM, VMEM],
        VMEM,
        [pltpu.VMEM((nb, cols), f32)],
    )(table, gathered, inverse, arrived, matrix)


def solution(mesh):
    return jax.shard_map(
        local,
        mesh=mesh,
        in_specs=(P("prow", "pcol"), P("prow", "pcol"), P()),
        out_specs=P("prow", "pcol"),
        check_vma=False,
    )
```

```python
from functools import partial

import jax
import jax.numpy as jnp
from jax import lax
from jax.experimental import pallas as pl
from jax.experimental.pallas import tpu as pltpu
from jax.sharding import PartitionSpec as P

HIGHEST = lax.Precision.HIGHEST
ROUND = 48
EARLY = 4
MAIN = 0
VMEM = pl.BlockSpec(memory_space=pltpu.VMEM)
HBM = pl.BlockSpec(memory_space=pltpu.HBM)
SMEM = pl.BlockSpec(memory_space=pltpu.SMEM)


def dot(a, b):
    return jnp.dot(a, b, precision=HIGHEST, preferred_element_type=jnp.float32)


class Table:
    ROW, PARTNER, PLACE, OWN, COUNT = range(5)


def spread_kernel(panel_ref, send_ref):
    nb = send_ref.shape[2]
    piece = panel_ref[:, :nb]
    for d in range(send_ref.shape[0]):
        send_ref[d] = piece


def join_kernel(panel_ref, pieces_ref, out_ref):
    rows = panel_ref.shape[1]
    out_ref[:, :rows] = panel_ref[...]
    out_ref[:, rows:] = pieces_ref[EARLY % pieces_ref.shape[0]]


def pack_kernel(pivots_ref, matrix_hbm, send_ref, table_ref, order_ref, count_ref, matrix_ref, sem):
    nb = pivots_ref.shape[0]
    rows = matrix_ref.shape[0]
    planes = count_ref.shape[0]
    room = send_ref.shape[0] // planes
    me = lax.axis_index("prow")
    bits = rows.bit_length() - 1
    fetch_matrix = pltpu.make_async_copy(matrix_hbm, matrix_ref, sem)
    fetch_matrix.start()

    def start(j, _):
        target = pivots_ref[j]
        order_ref[target] = target
        order_ref[j] = j
        return 0

    lax.fori_loop(0, nb, start, 0, unroll=16)

    def exchange(j, _):
        target = pivots_ref[j]
        first = order_ref[j]
        second = order_ref[target]
        order_ref[j] = second
        order_ref[target] = first
        return 0

    lax.fori_loop(0, nb, exchange, 0, unroll=16)
    for d in range(planes):
        count_ref[d] = 0

    def tally(i, _):
        row = order_ref[i]
        partner = order_ref[row]
        owner = row >> bits
        nth = count_ref[owner]
        count_ref[owner] = nth + 1
        table_ref[Table.ROW * nb + i] = row
        table_ref[Table.PARTNER * nb + i] = partner
        table_ref[Table.PLACE * nb + i] = ((owner + MAIN) & (planes - 1)) * room + jnp.minimum(nth, room - 1)
        table_ref[jnp.where(owner == me, Table.OWN * nb + nth, Table.COUNT * nb)] = i
        return 0

    lax.fori_loop(0, nb, tally, 0, unroll=16)
    table_ref[Table.COUNT * nb] = count_ref[me]
    most = count_ref[1]
    for d in range(2, planes):
        most = jnp.maximum(most, count_ref[d])
    table_ref[Table.COUNT * nb + 1] = jnp.where(count_ref[0] + most <= room, 1, 0)
    fetch_matrix.wait()

    def give(n, _):
        send_ref[pl.ds(n, 1), :] = matrix_ref[pl.ds(table_ref[Table.ROW * nb + table_ref[Table.OWN * nb + n]] & (rows - 1), 1), :]
        return 0

    lax.fori_loop(0, jnp.minimum(count_ref[me], room), give, 0)
    given = send_ref[:room, :]
    for d in range(1, planes):
        send_ref[d * room : (d + 1) * room, :] = given

    @pl.when(me == 0)
    def _():
        def hand(i, _):
            place = table_ref[Table.PLACE * nb + i]
            owner = table_ref[Table.ROW * nb + i] >> bits
            away = owner > 0
            partner = jnp.where(away, table_ref[Table.PARTNER * nb + i], 0)
            put = 2 * ((owner + MAIN) & (planes - 1)) * room + room - 1 - place
            put = jnp.where(away, put, MAIN * room + room - 1)
            send_ref[pl.ds(put, 1), :] = matrix_ref[pl.ds(partner, 1), :]
            return 0

        lax.fori_loop(0, nb, hand, 0, unroll=16)


def slot_kernel(table_ref, matrix_ref, send_ref):
    planes, slots, _ = send_ref.shape
    nb = planes * slots
    rows = matrix_ref.shape[0]
    me = lax.axis_index("prow")

    def place(d, _):
        for k in range(slots):
            i = d * slots + k
            mine = table_ref[Table.ROW * nb + i] - me * rows
            owned = (mine >= 0) & (mine < rows)
            take = jnp.where(owned, mine, jnp.where(me == 0, table_ref[Table.PARTNER * nb + i], 0))
            send_ref[d, k : k + 1, :] = matrix_ref[pl.ds(take, 1), :]
        return 0

    lax.fori_loop(0, planes, place, 0)


def sort_kernel(rows, table_ref, arrived_ref, send_ref):
    planes, slots, _ = arrived_ref.shape
    me = lax.axis_index("prow")
    for k in range(slots):
        owner = table_ref[me * slots + k] // rows
        send_ref[0, k : k + 1, :] = arrived_ref[owner, k : k + 1, :]
    send_ref[0, slots:, :] = arrived_ref[0]
    both = send_ref[0]
    for d in range(1, planes):
        send_ref[d] = both


def invert_upper(block):
    size = block.shape[0]
    row = lax.broadcasted_iota(jnp.int32, (size, size), 0)
    col = lax.broadcasted_iota(jnp.int32, (size, size), 1)
    inverse = None
    width = 1
    while width < size:
        pair = ((row ^ col) & ~(2 * width - 1)) == 0
        cross = jnp.where(pair & ((row & width) == 0) & ((col & width) != 0), block, 0.0)
        if inverse is None:
            inverse = jnp.where(row == col, 1.0, 0.0) - cross
        else:
            inverse = inverse - dot(dot(inverse, cross), inverse)
        width *= 2
    return inverse


def invert_kernel(gathered_ref, panel_ref, inverse_ref, lower_ref):
    rows, nb = panel_ref.shape
    half = nb // 2
    inverse_ref[:half] = invert_upper(gathered_ref[:half, rows : rows + half]).T
    inverse_ref[half:] = invert_upper(gathered_ref[half:, rows + half :]).T
    lower_ref[...] = gathered_ref[:half, rows + half :].T
    panel_ref[...] = gathered_ref[:, :rows].T


def update_kernel(one_round, table_ref, panel_ref, inverse_ref, lower_ref, arrived_ref, matrix_ref, out_ref, upper_ref):
    planes, slots, cols = upper_ref.shape
    nb = planes * slots
    rows = matrix_ref.shape[0]
    room = arrived_ref.shape[0] // planes
    half = nb // 2
    me = lax.axis_index("prow")

    def pick(d, _):
        for k in range(slots):
            place = table_ref[Table.PLACE * nb + d * slots + k] if one_round else d * room + k
            upper_ref[d, k : k + 1, :] = arrived_ref[pl.ds(place, 1), :]
        return 0

    lax.fori_loop(0, planes, pick, 0)
    out_ref[...] = matrix_ref[...]

    def patch(n, _):
        slot = table_ref[Table.OWN * nb + n]
        if one_round:
            place = MAIN * room + jnp.where(me == 0, 0, room - 1 - n)
        else:
            place = slot // slots * room + slots + slot % slots
        far = arrived_ref[pl.ds(place, 1), :]
        lands = jnp.where(me == 0, jnp.minimum(table_ref[Table.PARTNER * nb + slot], rows - 1), 0)
        near = matrix_ref[pl.ds(lands, 1), :]
        out_ref[pl.ds(table_ref[Table.ROW * nb + slot] - me * rows, 1), :] = jnp.where(me == 0, near, far)
        return 0

    lax.fori_loop(0, table_ref[Table.COUNT * nb], patch, 0)
    upper = upper_ref[...].reshape(nb, cols)
    top = dot(inverse_ref[:half], upper[:half])
    rest = upper[half:] - dot(lower_ref[...], top)
    upper = jnp.concatenate([top, dot(inverse_ref[half:], rest)], axis=0)
    out_ref[...] -= dot(panel_ref[...], upper)

    @pl.when(me == 0)
    def _():
        out_ref[:nb, :] = upper


def call(kernel, outs, in_specs, out_specs, scratch=()):
    return pl.pallas_call(
        kernel,
        out_shape=outs,
        in_specs=in_specs,
        out_specs=out_specs,
        scratch_shapes=list(scratch),
        compiler_params=pltpu.CompilerParams(vmem_limit_bytes=16 * 1024 * 1024),
    )


def exchange(value, place):
    planes = value.shape[0]
    order = [[(p - place) % planes for p in range(planes)]]
    return lax.all_to_all(value, "prow", 0, 0, axis_index_groups=order)


def local(matrix, factored_panel, pivots):
    rows, cols = matrix.shape
    nb = pivots.shape[0]
    planes = lax.axis_size("prow")
    slots = nb // planes
    width = factored_panel.shape[1]
    room = min(ROUND, nb)
    f32 = jnp.float32
    panel = factored_panel.T
    pieces = call(spread_kernel, jax.ShapeDtypeStruct((planes, width, nb), f32), [VMEM], VMEM)(panel)
    pieces = exchange(pieces, EARLY)
    send, table = call(
        pack_kernel,
        (
            jax.ShapeDtypeStruct((planes * room, cols), f32),
            jax.ShapeDtypeStruct((8 * nb,), jnp.int32),
        ),
        [SMEM, HBM],
        (VMEM, SMEM),
        [
            pltpu.SMEM((rows * planes,), jnp.int32),
            pltpu.SMEM((planes,), jnp.int32),
            pltpu.VMEM((rows, cols), f32),
            pltpu.SemaphoreType.DMA,
        ],
    )(pivots, matrix)

    def finish(one_round, table, panel, pieces, arrived, matrix):
        pieces = call(join_kernel, jax.ShapeDtypeStruct((width, rows + nb), f32), [VMEM, VMEM], VMEM)(panel, pieces)
        gathered = lax.all_gather(pieces, "pcol", axis=0, tiled=True)
        by_rows = call(
            invert_kernel,
            (
                jax.ShapeDtypeStruct((rows, nb), f32),
                jax.ShapeDtypeStruct((nb, nb // 2), f32),
                jax.ShapeDtypeStruct((nb // 2, nb // 2), f32),
            ),
            [VMEM],
            (VMEM, VMEM, VMEM),
        )(gathered)
        return call(
            partial(update_kernel, one_round),
            jax.ShapeDtypeStruct((rows, cols), f32),
            [SMEM, VMEM, VMEM, VMEM, VMEM, VMEM],
            VMEM,
            [pltpu.VMEM((planes, slots, cols), f32)],
        )(table, *by_rows, arrived, matrix)

    def one_round(send, table, panel, pieces, matrix):
        arrived = exchange(send.reshape(planes, room, cols), MAIN)
        return finish(True, table, panel, pieces, arrived.reshape(planes * room, cols), matrix)

    def two_rounds(send, table, panel, pieces, matrix):
        slot = jax.ShapeDtypeStruct((planes, slots, cols), f32)
        both = jax.ShapeDtypeStruct((planes, 2 * slots, cols), f32)
        arrived = exchange(call(slot_kernel, slot, [SMEM, VMEM], VMEM)(table, matrix), 0)
        send = call(partial(sort_kernel, rows), both, [SMEM, VMEM], VMEM)(table, arrived)
        arrived = exchange(send, 0)
        return finish(False, table, panel, pieces, arrived.reshape(2 * nb, cols), matrix)

    fits = table[Table.COUNT * nb + 1] == 1
    return lax.cond(fits, one_round, two_rounds, send, table, panel, pieces, matrix)


def solution(mesh):
    return jax.shard_map(
        local,
        mesh=mesh,
        in_specs=(P("prow", "pcol"), P("prow", "pcol"), P()),
        out_specs=P("prow", "pcol"),
        check_vma=False,
    )
```

```python
from functools import partial

import jax
import jax.numpy as jnp
from jax import lax
from jax.experimental import pallas as pl
from jax.experimental.pallas import tpu as pltpu
from jax.sharding import PartitionSpec as P

HIGHEST = lax.Precision.HIGHEST
ROUNDS = (40, 48)
EARLY = 4
MAIN = 4
VMEM = pl.BlockSpec(memory_space=pltpu.VMEM)
HBM = pl.BlockSpec(memory_space=pltpu.HBM)
SMEM = pl.BlockSpec(memory_space=pltpu.SMEM)


def dot(a, b):
    return jnp.dot(a, b, precision=HIGHEST, preferred_element_type=jnp.float32)


class Table:
    ROW, PARTNER, PLACE, OWN, COUNT = range(5)


def spread_kernel(panel_ref, send_ref):
    nb = send_ref.shape[2]
    piece = panel_ref[:, :nb]
    for d in range(send_ref.shape[0]):
        send_ref[d] = piece


def join_kernel(panel_ref, pieces_ref, out_ref):
    rows = panel_ref.shape[1]
    out_ref[:, :rows] = panel_ref[...]
    out_ref[:, rows:] = pieces_ref[EARLY % pieces_ref.shape[0]]


def pack_kernel(pivots_ref, matrix_hbm, *refs):
    *send_refs, table_ref, order_ref, count_ref, matrix_ref, sem = refs
    nb = pivots_ref.shape[0]
    rows = matrix_ref.shape[0]
    planes = count_ref.shape[0]
    rooms = [send_ref.shape[0] // planes for send_ref in send_refs]
    me = lax.axis_index("prow")
    bits = rows.bit_length() - 1
    fetch_matrix = pltpu.make_async_copy(matrix_hbm, matrix_ref, sem)
    fetch_matrix.start()

    def start(j, _):
        target = pivots_ref[j]
        order_ref[target] = target
        order_ref[j] = j
        return 0

    lax.fori_loop(0, nb, start, 0, unroll=16)

    for d in range(planes):
        count_ref[d] = 0

    def exchange(j, _):
        target = pivots_ref[j]
        first = order_ref[j]
        row = order_ref[target]
        order_ref[target] = first
        table_ref[Table.ROW * nb + j] = row
        owner = row >> bits
        nth = count_ref[owner]
        count_ref[owner] = nth + 1
        table_ref[Table.PLACE * nb + j] = (((owner + MAIN) & (planes - 1)) << 8) + nth
        table_ref[jnp.where(owner == me, Table.OWN * nb + nth, Table.COUNT * nb)] = j
        return 0

    lax.fori_loop(0, nb, exchange, 0, unroll=16)
    table_ref[Table.COUNT * nb] = count_ref[me]
    most = count_ref[1]
    for d in range(2, planes):
        most = jnp.maximum(most, count_ref[d])

    @pl.when(me == 0)
    def _():
        def meet(i, _):
            table_ref[Table.PARTNER * nb + i] = order_ref[table_ref[Table.ROW * nb + i]]
            return 0

        lax.fori_loop(0, nb, meet, 0, unroll=16)

    most = count_ref[0] + most
    level = len(rooms)
    for n in reversed(range(len(rooms))):
        level = jnp.where(most <= rooms[n], n, level)
    table_ref[Table.COUNT * nb + 1] = level
    fetch_matrix.wait()

    def fill(send_ref, room):
        def give(n, _):
            mine = table_ref[Table.ROW * nb + table_ref[Table.OWN * nb + n]] & (rows - 1)
            send_ref[pl.ds(n, 1), :] = matrix_ref[pl.ds(mine, 1), :]
            return 0

        lax.fori_loop(0, count_ref[me], give, 0)
        given = send_ref[:room, :]
        for d in range(1, planes):
            send_ref[d * room : (d + 1) * room, :] = given

        @pl.when(me == 0)
        def _():
            def hand(i, _):
                place = table_ref[Table.PLACE * nb + i]
                away = table_ref[Table.ROW * nb + i] >= rows
                partner = jnp.where(away, table_ref[Table.PARTNER * nb + i], 0)
                put = jnp.where(away, ((place >> 8) + 1) * room - (place & 255), (MAIN + 1) * room) - 1
                send_ref[pl.ds(put, 1), :] = matrix_ref[pl.ds(partner, 1), :]
                return 0

            lax.fori_loop(0, nb, hand, 0, unroll=16)

    for n, send_ref in enumerate(send_refs):
        pl.when(level == n)(partial(fill, send_ref, rooms[n]))


def slot_kernel(table_ref, matrix_ref, send_ref):
    planes, slots, _ = send_ref.shape
    nb = planes * slots
    rows = matrix_ref.shape[0]
    me = lax.axis_index("prow")

    def place(d, _):
        for k in range(slots):
            i = d * slots + k
            mine = table_ref[Table.ROW * nb + i] - me * rows
            owned = (mine >= 0) & (mine < rows)
            take = jnp.where(owned, mine, jnp.where(me == 0, table_ref[Table.PARTNER * nb + i], 0))
            send_ref[d, k : k + 1, :] = matrix_ref[pl.ds(take, 1), :]
        return 0

    lax.fori_loop(0, planes, place, 0)


def sort_kernel(rows, table_ref, arrived_ref, send_ref):
    planes, slots, _ = arrived_ref.shape
    me = lax.axis_index("prow")
    for k in range(slots):
        owner = table_ref[me * slots + k] // rows
        send_ref[0, k : k + 1, :] = arrived_ref[owner, k : k + 1, :]
    send_ref[0, slots:, :] = arrived_ref[0]
    both = send_ref[0]
    for d in range(1, planes):
        send_ref[d] = both


def invert_upper(block):
    size = block.shape[0]
    row = lax.broadcasted_iota(jnp.int32, (size, size), 0)
    col = lax.broadcasted_iota(jnp.int32, (size, size), 1)
    inverse = None
    width = 1
    while width < size:
        pair = ((row ^ col) & ~(2 * width - 1)) == 0
        cross = jnp.where(pair & ((row & width) == 0) & ((col & width) != 0), block, 0.0)
        if inverse is None:
            inverse = jnp.where(row == col, 1.0, 0.0) - cross
        else:
            inverse = inverse - dot(dot(inverse, cross), inverse)
        width *= 2
    return inverse


def invert_kernel(gathered_ref, panel_ref, inverse_ref, lower_ref):
    rows, nb = panel_ref.shape
    half = nb // 2
    inverse_ref[:half] = invert_upper(gathered_ref[:half, rows : rows + half]).T
    inverse_ref[half:] = invert_upper(gathered_ref[half:, rows + half :]).T
    lower_ref[...] = gathered_ref[:half, rows + half :].T
    panel_ref[...] = gathered_ref[:, :rows].T


def update_kernel(one_round, table_ref, panel_ref, inverse_ref, lower_ref, arrived_ref, matrix_ref, out_ref, upper_ref):
    planes, slots, cols = upper_ref.shape
    nb = planes * slots
    rows = matrix_ref.shape[0]
    room = arrived_ref.shape[0] // planes
    half = nb // 2
    me = lax.axis_index("prow")

    def pick(d, _):
        for k in range(slots):
            place = d * room + k
            if one_round:
                place = table_ref[Table.PLACE * nb + d * slots + k]
                place = (place >> 8) * room + (place & 255)
            upper_ref[d, k : k + 1, :] = arrived_ref[pl.ds(place, 1), :]
        return 0

    lax.fori_loop(0, planes, pick, 0)
    out_ref[...] = matrix_ref[...]

    def patch(n, _):
        slot = table_ref[Table.OWN * nb + n]
        if one_round:
            place = MAIN * room + jnp.where(me == 0, 0, room - 1 - n)
        else:
            place = slot // slots * room + slots + slot % slots
        far = arrived_ref[pl.ds(place, 1), :]
        lands = jnp.where(me == 0, jnp.minimum(table_ref[Table.PARTNER * nb + slot], rows - 1), 0)
        near = matrix_ref[pl.ds(lands, 1), :]
        out_ref[pl.ds(table_ref[Table.ROW * nb + slot] - me * rows, 1), :] = jnp.where(me == 0, near, far)
        return 0

    lax.fori_loop(0, table_ref[Table.COUNT * nb], patch, 0)
    upper = upper_ref[...].reshape(nb, cols)
    top = dot(inverse_ref[:half], upper[:half])
    rest = upper[half:] - dot(lower_ref[...], top)
    upper = jnp.concatenate([top, dot(inverse_ref[half:], rest)], axis=0)
    out_ref[...] -= dot(panel_ref[...], upper)

    @pl.when(me == 0)
    def _():
        out_ref[:nb, :] = upper


def call(kernel, outs, in_specs, out_specs, scratch=()):
    return pl.pallas_call(
        kernel,
        out_shape=outs,
        in_specs=in_specs,
        out_specs=out_specs,
        scratch_shapes=list(scratch),
        compiler_params=pltpu.CompilerParams(vmem_limit_bytes=16 * 1024 * 1024),
    )


def exchange(value, place):
    planes = value.shape[0]
    order = [[(p - place) % planes for p in range(planes)]]
    return lax.all_to_all(value, "prow", 0, 0, axis_index_groups=order)


def local(matrix, factored_panel, pivots):
    rows, cols = matrix.shape
    nb = pivots.shape[0]
    planes = lax.axis_size("prow")
    slots = nb // planes
    width = factored_panel.shape[1]
    rooms = ROUNDS
    f32 = jnp.float32
    panel = factored_panel.T
    pieces = call(spread_kernel, jax.ShapeDtypeStruct((planes, width, nb), f32), [VMEM], VMEM)(panel)
    pieces = exchange(pieces, EARLY)
    *sends, table = call(
        pack_kernel,
        (
            *(jax.ShapeDtypeStruct((planes * room, cols), f32) for room in rooms),
            jax.ShapeDtypeStruct((8 * nb,), jnp.int32),
        ),
        [SMEM, HBM],
        (*(VMEM for _ in rooms), SMEM),
        [
            pltpu.SMEM((rows * planes,), jnp.int32),
            pltpu.SMEM((planes,), jnp.int32),
            pltpu.VMEM((rows, cols), f32),
            pltpu.SemaphoreType.DMA,
        ],
    )(pivots, matrix)

    def finish(one_round, table, panel, pieces, arrived, matrix):
        pieces = call(join_kernel, jax.ShapeDtypeStruct((width, rows + nb), f32), [VMEM, VMEM], VMEM)(panel, pieces)
        gathered = lax.all_gather(pieces, "pcol", axis=0, tiled=True)
        by_rows = call(
            invert_kernel,
            (
                jax.ShapeDtypeStruct((rows, nb), f32),
                jax.ShapeDtypeStruct((nb, nb // 2), f32),
                jax.ShapeDtypeStruct((nb // 2, nb // 2), f32),
            ),
            [VMEM],
            (VMEM, VMEM, VMEM),
        )(gathered)
        return call(
            partial(update_kernel, one_round),
            jax.ShapeDtypeStruct((rows, cols), f32),
            [SMEM, VMEM, VMEM, VMEM, VMEM, VMEM],
            VMEM,
            [pltpu.VMEM((planes, slots, cols), f32)],
        )(table, *by_rows, arrived, matrix)

    def one_round(level, sends, table, panel, pieces, matrix):
        arrived = exchange(sends[level].reshape(planes, rooms[level], cols), MAIN)
        return finish(True, table, panel, pieces, arrived.reshape(planes * rooms[level], cols), matrix)

    def two_rounds(sends, table, panel, pieces, matrix):
        slot = jax.ShapeDtypeStruct((planes, slots, cols), f32)
        both = jax.ShapeDtypeStruct((planes, 2 * slots, cols), f32)
        arrived = exchange(call(slot_kernel, slot, [SMEM, VMEM], VMEM)(table, matrix), 0)
        send = call(partial(sort_kernel, rows), both, [SMEM, VMEM], VMEM)(table, arrived)
        arrived = exchange(send, 0)
        return finish(False, table, panel, pieces, arrived.reshape(2 * nb, cols), matrix)

    forms = [*(partial(one_round, level) for level in range(len(rooms))), two_rounds]
    return lax.switch(table[Table.COUNT * nb + 1], forms, sends, table, panel, pieces, matrix)


def solution(mesh):
    return jax.shard_map(
        local,
        mesh=mesh,
        in_specs=(P("prow", "pcol"), P("prow", "pcol"), P()),
        out_specs=P("prow", "pcol"),
        check_vma=False,
    )
```

```python
from functools import partial

import jax
import jax.numpy as jnp
from jax import lax
from jax.experimental import pallas as pl
from jax.experimental.pallas import tpu as pltpu
from jax.sharding import PartitionSpec as P

HIGHEST = lax.Precision.HIGHEST
ROUNDS = (40, 48)
EARLY = 4
MAIN = 4
VMEM = pl.BlockSpec(memory_space=pltpu.VMEM)
HBM = pl.BlockSpec(memory_space=pltpu.HBM)
SMEM = pl.BlockSpec(memory_space=pltpu.SMEM)


def dot(a, b):
    return jnp.dot(a, b, precision=HIGHEST, preferred_element_type=jnp.float32)


class Table:
    ROW, PARTNER, OWN, COUNT, PLACE = range(5)


def spread_kernel(panel_ref, send_ref):
    nb = send_ref.shape[2]
    piece = panel_ref[:, :nb]
    for d in range(send_ref.shape[0]):
        send_ref[d] = piece


def join_kernel(panel_ref, pieces_ref, out_ref):
    rows = panel_ref.shape[1]
    out_ref[:, :rows] = panel_ref[...]
    out_ref[:, rows:] = pieces_ref[EARLY % pieces_ref.shape[0]]


def pack_kernel(pivots_ref, matrix_hbm, *refs):
    *send_refs, table_ref, order_ref, fill_ref, matrix_ref, sem = refs
    nb = pivots_ref.shape[0]
    rows = matrix_ref.shape[0]
    planes = fill_ref.shape[0] // len(send_refs)
    rooms = [send_ref.shape[0] // planes for send_ref in send_refs]
    me = lax.axis_index("prow")
    bits = rows.bit_length() - 1
    fetch_matrix = pltpu.make_async_copy(matrix_hbm, matrix_ref, sem)
    fetch_matrix.start()

    def start(j, _):
        target = pivots_ref[j]
        order_ref[target] = target
        order_ref[j] = j
        return 0

    lax.fori_loop(0, nb, start, 0, unroll=16)

    def first_place(plane, room):
        return ((plane + MAIN) & (planes - 1)) * room

    for d in range(planes):
        for n, room in enumerate(rooms):
            fill_ref[n * planes + d] = first_place(d, room)

    mine_from = first_place(me, rooms[0])

    def exchange(j, _):
        target = pivots_ref[j]
        first = order_ref[j]
        row = order_ref[target]
        order_ref[target] = first
        table_ref[Table.ROW * nb + j] = row
        owner = row >> bits
        for n in range(len(rooms)):
            place = fill_ref[n * planes + owner]
            fill_ref[n * planes + owner] = place + 1
            table_ref[(Table.PLACE + n) * nb + j] = place
            if n == 0:
                own = Table.OWN * nb - mine_from + place
        table_ref[jnp.where(owner == me, own, Table.COUNT * nb)] = j
        return 0

    lax.fori_loop(0, nb, exchange, 0, unroll=16)
    count = fill_ref[me] - mine_from
    table_ref[Table.COUNT * nb] = count
    most = 0
    for d in range(1, planes):
        most = jnp.maximum(most, fill_ref[d] - first_place(d, rooms[0]))

    @pl.when(me == 0)
    def _():
        def meet(i, _):
            table_ref[Table.PARTNER * nb + i] = order_ref[table_ref[Table.ROW * nb + i]]
            return 0

        lax.fori_loop(0, nb, meet, 0, unroll=16)

    most = fill_ref[0] - first_place(0, rooms[0]) + most
    level = len(rooms)
    for n in reversed(range(len(rooms))):
        level = jnp.where(most <= rooms[n], n, level)
    table_ref[Table.COUNT * nb + 1] = level
    fetch_matrix.wait()

    def fill(n, send_ref, room):
        def give(k, _):
            mine = table_ref[Table.ROW * nb + table_ref[Table.OWN * nb + k]] & (rows - 1)
            send_ref[pl.ds(k, 1), :] = matrix_ref[pl.ds(mine, 1), :]
            return 0

        lax.fori_loop(0, count, give, 0)
        given = send_ref[:room, :]
        for d in range(1, planes):
            send_ref[d * room : (d + 1) * room, :] = given

        @pl.when(me == 0)
        def _():
            def hand(i, _):
                row = table_ref[Table.ROW * nb + i]
                away = row >= rows
                partner = jnp.where(away, table_ref[Table.PARTNER * nb + i], 0)
                put = 2 * first_place(row >> bits, room) + room - 1 - table_ref[(Table.PLACE + n) * nb + i]
                put = jnp.where(away, put, (MAIN + 1) * room - 1)
                send_ref[pl.ds(put, 1), :] = matrix_ref[pl.ds(partner, 1), :]
                return 0

            lax.fori_loop(0, nb, hand, 0, unroll=16)

    for n, send_ref in enumerate(send_refs):
        pl.when(level == n)(partial(fill, n, send_ref, rooms[n]))


def slot_kernel(table_ref, matrix_ref, send_ref):
    planes, slots, _ = send_ref.shape
    nb = planes * slots
    rows = matrix_ref.shape[0]
    me = lax.axis_index("prow")

    def place(d, _):
        for k in range(slots):
            i = d * slots + k
            mine = table_ref[Table.ROW * nb + i] - me * rows
            owned = (mine >= 0) & (mine < rows)
            take = jnp.where(owned, mine, jnp.where(me == 0, table_ref[Table.PARTNER * nb + i], 0))
            send_ref[d, k : k + 1, :] = matrix_ref[pl.ds(take, 1), :]
        return 0

    lax.fori_loop(0, planes, place, 0)


def sort_kernel(rows, table_ref, arrived_ref, send_ref):
    planes, slots, _ = arrived_ref.shape
    me = lax.axis_index("prow")
    for k in range(slots):
        owner = table_ref[me * slots + k] // rows
        send_ref[0, k : k + 1, :] = arrived_ref[owner, k : k + 1, :]
    send_ref[0, slots:, :] = arrived_ref[0]
    both = send_ref[0]
    for d in range(1, planes):
        send_ref[d] = both


def invert_upper(block):
    size = block.shape[0]
    row = lax.broadcasted_iota(jnp.int32, (size, size), 0)
    col = lax.broadcasted_iota(jnp.int32, (size, size), 1)
    inverse = None
    width = 1
    while width < size:
        pair = ((row ^ col) & ~(2 * width - 1)) == 0
        cross = jnp.where(pair & ((row & width) == 0) & ((col & width) != 0), block, 0.0)
        if inverse is None:
            inverse = jnp.where(row == col, 1.0, 0.0) - cross
        else:
            inverse = inverse - dot(dot(inverse, cross), inverse)
        width *= 2
    return inverse


def invert_kernel(gathered_ref, panel_ref, inverse_ref, lower_ref):
    rows, nb = panel_ref.shape
    half = nb // 2
    inverse_ref[:half] = invert_upper(gathered_ref[:half, rows : rows + half]).T
    inverse_ref[half:] = invert_upper(gathered_ref[half:, rows + half :]).T
    lower_ref[...] = gathered_ref[:half, rows + half :].T
    panel_ref[...] = gathered_ref[:, :rows].T


def update_kernel(level, table_ref, panel_ref, inverse_ref, lower_ref, arrived_ref, matrix_ref, out_ref, upper_ref):
    planes, slots, cols = upper_ref.shape
    nb = planes * slots
    rows = matrix_ref.shape[0]
    room = arrived_ref.shape[0] // planes
    half = nb // 2
    me = lax.axis_index("prow")

    def pick(d, _):
        for k in range(slots):
            place = d * room + k
            if level is not None:
                place = table_ref[(Table.PLACE + level) * nb + d * slots + k]
            upper_ref[d, k : k + 1, :] = arrived_ref[pl.ds(place, 1), :]
        return 0

    lax.fori_loop(0, planes, pick, 0)
    out_ref[...] = matrix_ref[...]

    def patch(n, _):
        slot = table_ref[Table.OWN * nb + n]
        if level is not None:
            place = MAIN * room + jnp.where(me == 0, 0, room - 1 - n)
        else:
            place = slot // slots * room + slots + slot % slots
        far = arrived_ref[pl.ds(place, 1), :]
        lands = jnp.where(me == 0, jnp.minimum(table_ref[Table.PARTNER * nb + slot], rows - 1), 0)
        near = matrix_ref[pl.ds(lands, 1), :]
        out_ref[pl.ds(table_ref[Table.ROW * nb + slot] - me * rows, 1), :] = jnp.where(me == 0, near, far)
        return 0

    lax.fori_loop(0, table_ref[Table.COUNT * nb], patch, 0)
    upper = upper_ref[...].reshape(nb, cols)
    top = dot(inverse_ref[:half], upper[:half])
    rest = upper[half:] - dot(lower_ref[...], top)
    upper = jnp.concatenate([top, dot(inverse_ref[half:], rest)], axis=0)
    out_ref[...] -= dot(panel_ref[...], upper)

    @pl.when(me == 0)
    def _():
        out_ref[:nb, :] = upper


def call(kernel, outs, in_specs, out_specs, scratch=()):
    return pl.pallas_call(
        kernel,
        out_shape=outs,
        in_specs=in_specs,
        out_specs=out_specs,
        scratch_shapes=list(scratch),
        compiler_params=pltpu.CompilerParams(vmem_limit_bytes=16 * 1024 * 1024),
    )


def exchange(value, place):
    planes = value.shape[0]
    order = [[(p - place) % planes for p in range(planes)]]
    return lax.all_to_all(value, "prow", 0, 0, axis_index_groups=order)


def local(matrix, factored_panel, pivots):
    rows, cols = matrix.shape
    nb = pivots.shape[0]
    planes = lax.axis_size("prow")
    slots = nb // planes
    width = factored_panel.shape[1]
    rooms = ROUNDS
    f32 = jnp.float32
    panel = factored_panel.T
    pieces = call(spread_kernel, jax.ShapeDtypeStruct((planes, width, nb), f32), [VMEM], VMEM)(panel)
    pieces = exchange(pieces, EARLY)
    *sends, table = call(
        pack_kernel,
        (
            *(jax.ShapeDtypeStruct((planes * room, cols), f32) for room in rooms),
            jax.ShapeDtypeStruct((8 * nb,), jnp.int32),
        ),
        [SMEM, HBM],
        (*(VMEM for _ in rooms), SMEM),
        [
            pltpu.SMEM((rows * planes,), jnp.int32),
            pltpu.SMEM((len(rooms) * planes,), jnp.int32),
            pltpu.VMEM((rows, cols), f32),
            pltpu.SemaphoreType.DMA,
        ],
    )(pivots, matrix)

    def finish(level, table, panel, pieces, arrived, matrix):
        pieces = call(join_kernel, jax.ShapeDtypeStruct((width, rows + nb), f32), [VMEM, VMEM], VMEM)(panel, pieces)
        gathered = lax.all_gather(pieces, "pcol", axis=0, tiled=True)
        by_rows = call(
            invert_kernel,
            (
                jax.ShapeDtypeStruct((rows, nb), f32),
                jax.ShapeDtypeStruct((nb, nb // 2), f32),
                jax.ShapeDtypeStruct((nb // 2, nb // 2), f32),
            ),
            [VMEM],
            (VMEM, VMEM, VMEM),
        )(gathered)
        return call(
            partial(update_kernel, level),
            jax.ShapeDtypeStruct((rows, cols), f32),
            [SMEM, VMEM, VMEM, VMEM, VMEM, VMEM],
            VMEM,
            [pltpu.VMEM((planes, slots, cols), f32)],
        )(table, *by_rows, arrived, matrix)

    def one_round(level, sends, table, panel, pieces, matrix):
        arrived = exchange(sends[level].reshape(planes, rooms[level], cols), MAIN)
        return finish(level, table, panel, pieces, arrived.reshape(planes * rooms[level], cols), matrix)

    def two_rounds(sends, table, panel, pieces, matrix):
        slot = jax.ShapeDtypeStruct((planes, slots, cols), f32)
        both = jax.ShapeDtypeStruct((planes, 2 * slots, cols), f32)
        arrived = exchange(call(slot_kernel, slot, [SMEM, VMEM], VMEM)(table, matrix), 0)
        send = call(partial(sort_kernel, rows), both, [SMEM, VMEM], VMEM)(table, arrived)
        arrived = exchange(send, 0)
        return finish(None, table, panel, pieces, arrived.reshape(2 * nb, cols), matrix)

    forms = [*(partial(one_round, level) for level in range(len(rooms))), two_rounds]
    return lax.switch(table[Table.COUNT * nb + 1], forms, sends, table, panel, pieces, matrix)


def solution(mesh):
    return jax.shard_map(
        local,
        mesh=mesh,
        in_specs=(P("prow", "pcol"), P("prow", "pcol"), P()),
        out_specs=P("prow", "pcol"),
        check_vma=False,
    )
```

```python
from functools import partial

import jax
import jax.numpy as jnp
from jax import lax
from jax.experimental import pallas as pl
from jax.experimental.pallas import tpu as pltpu
from jax.sharding import PartitionSpec as P

HIGHEST = lax.Precision.HIGHEST
ROUNDS = (40, 48)
EARLY = 4
MAIN = 4
VMEM = pl.BlockSpec(memory_space=pltpu.VMEM)
HBM = pl.BlockSpec(memory_space=pltpu.HBM)
SMEM = pl.BlockSpec(memory_space=pltpu.SMEM)


def dot(a, b):
    return jnp.dot(a, b, precision=HIGHEST, preferred_element_type=jnp.float32)


class Table:
    ROW, PARTNER, OWN, COUNT, PLACE = range(5)


def spread_kernel(panel_ref, send_ref):
    nb = send_ref.shape[2]
    piece = panel_ref[:, :nb]
    for d in range(send_ref.shape[0]):
        send_ref[d] = piece


def join_kernel(panel_ref, pieces_ref, out_ref):
    rows = panel_ref.shape[1]
    out_ref[:, :rows] = panel_ref[...]
    out_ref[:, rows:] = pieces_ref[EARLY % pieces_ref.shape[0]]


def pack_kernel(pivots_ref, matrix_hbm, *refs):
    *send_refs, level_ref, table_ref, order_ref, fill_ref, matrix_ref, sem = refs
    nb = pivots_ref.shape[0]
    rows = matrix_ref.shape[0]
    planes = fill_ref.shape[0] // len(send_refs)
    rooms = [send_ref.shape[0] // planes for send_ref in send_refs]
    me = lax.axis_index("prow")
    bits = rows.bit_length() - 1
    fetch_matrix = pltpu.make_async_copy(matrix_hbm, matrix_ref, sem)
    fetch_matrix.start()

    def start(j, _):
        target = pivots_ref[j]
        order_ref[target] = target
        order_ref[j] = j
        return 0

    lax.fori_loop(0, nb, start, 0, unroll=16)

    def first_place(plane, room):
        return ((plane + MAIN) & (planes - 1)) * room

    for d in range(planes):
        for n, room in enumerate(rooms):
            fill_ref[n * planes + d] = first_place(d, room)

    mine_from = first_place(me, rooms[0])

    def exchange(j, _):
        target = pivots_ref[j]
        first = order_ref[j]
        row = order_ref[target]
        order_ref[target] = first
        table_ref[Table.ROW * nb + j] = row
        owner = row >> bits
        for n in range(len(rooms)):
            place = fill_ref[n * planes + owner]
            fill_ref[n * planes + owner] = place + 1
            table_ref[(Table.PLACE + n) * nb + j] = place
            if n == 0:
                own = Table.OWN * nb - mine_from + place
        table_ref[jnp.where(owner == me, own, Table.COUNT * nb)] = j
        return 0

    lax.fori_loop(0, nb, exchange, 0, unroll=16)
    count = fill_ref[me] - mine_from
    table_ref[Table.COUNT * nb] = count
    most = 0
    for d in range(1, planes):
        most = jnp.maximum(most, fill_ref[d] - first_place(d, rooms[0]))

    most = fill_ref[0] - first_place(0, rooms[0]) + most
    level = len(rooms)
    for n in reversed(range(len(rooms))):
        level = jnp.where(most <= rooms[n], n, level)
    level_ref[0] = level

    @pl.when((me == 0) & (level == len(rooms)))
    def _():
        def meet(i, _):
            table_ref[Table.PARTNER * nb + i] = order_ref[table_ref[Table.ROW * nb + i]]
            return 0

        lax.fori_loop(0, nb, meet, 0, unroll=16)

    fetch_matrix.wait()

    def fill(n, send_ref, room):
        def give(k, _):
            slot = table_ref[Table.OWN * nb + k]
            row = table_ref[Table.ROW * nb + slot]
            table_ref[Table.PARTNER * nb + slot] = order_ref[row]
            mine = row & (rows - 1)
            send_ref[pl.ds(k, 1), :] = matrix_ref[pl.ds(mine, 1), :]
            return 0

        lax.fori_loop(0, count, give, 0)
        given = send_ref[:room, :]
        for d in range(1, planes):
            send_ref[d * room : (d + 1) * room, :] = given

        @pl.when(me == 0)
        def _():
            def hand(i, _):
                row = table_ref[Table.ROW * nb + i]
                away = row >= rows
                partner = jnp.where(away, order_ref[row], 0)
                put = 2 * first_place(row >> bits, room) + room - 1 - table_ref[(Table.PLACE + n) * nb + i]
                put = jnp.where(away, put, (MAIN + 1) * room - 1)
                send_ref[pl.ds(put, 1), :] = matrix_ref[pl.ds(partner, 1), :]
                return 0

            lax.fori_loop(0, nb, hand, 0, unroll=16)

    for n, send_ref in enumerate(send_refs):
        pl.when(level == n)(partial(fill, n, send_ref, rooms[n]))


def slot_kernel(table_ref, matrix_ref, send_ref):
    planes, slots, _ = send_ref.shape
    nb = planes * slots
    rows = matrix_ref.shape[0]
    me = lax.axis_index("prow")

    def place(d, _):
        for k in range(slots):
            i = d * slots + k
            mine = table_ref[Table.ROW * nb + i] - me * rows
            owned = (mine >= 0) & (mine < rows)
            take = jnp.where(owned, mine, jnp.where(me == 0, table_ref[Table.PARTNER * nb + i], 0))
            send_ref[d, k : k + 1, :] = matrix_ref[pl.ds(take, 1), :]
        return 0

    lax.fori_loop(0, planes, place, 0)


def sort_kernel(rows, table_ref, arrived_ref, send_ref):
    planes, slots, _ = arrived_ref.shape
    me = lax.axis_index("prow")
    for k in range(slots):
        owner = table_ref[me * slots + k] // rows
        send_ref[0, k : k + 1, :] = arrived_ref[owner, k : k + 1, :]
    send_ref[0, slots:, :] = arrived_ref[0]
    both = send_ref[0]
    for d in range(1, planes):
        send_ref[d] = both


def invert_upper(block):
    size = block.shape[0]
    row = lax.broadcasted_iota(jnp.int32, (size, size), 0)
    col = lax.broadcasted_iota(jnp.int32, (size, size), 1)
    inverse = None
    width = 1
    while width < size:
        pair = ((row ^ col) & ~(2 * width - 1)) == 0
        cross = jnp.where(pair & ((row & width) == 0) & ((col & width) != 0), block, 0.0)
        if inverse is None:
            inverse = jnp.where(row == col, 1.0, 0.0) - cross
        else:
            inverse = inverse - dot(dot(inverse, cross), inverse)
        width *= 2
    return inverse


def invert_kernel(gathered_ref, panel_ref, inverse_ref, lower_ref):
    rows, nb = panel_ref.shape
    half = nb // 2
    inverse_ref[:half] = invert_upper(gathered_ref[:half, rows : rows + half]).T
    inverse_ref[half:] = invert_upper(gathered_ref[half:, rows + half :]).T
    lower_ref[...] = gathered_ref[:half, rows + half :].T
    panel_ref[...] = gathered_ref[:, :rows].T


def update_kernel(level, table_ref, panel_ref, inverse_ref, lower_ref, arrived_ref, matrix_ref, out_ref, upper_ref):
    planes, slots, cols = upper_ref.shape
    nb = planes * slots
    rows = matrix_ref.shape[0]
    room = arrived_ref.shape[0] // planes
    half = nb // 2
    me = lax.axis_index("prow")

    def pick(d, _):
        for k in range(slots):
            place = d * room + k
            if level is not None:
                place = table_ref[(Table.PLACE + level) * nb + d * slots + k]
            upper_ref[d, k : k + 1, :] = arrived_ref[pl.ds(place, 1), :]
        return 0

    lax.fori_loop(0, planes, pick, 0)
    out_ref[...] = matrix_ref[...]

    def patch(n, _):
        slot = table_ref[Table.OWN * nb + n]
        if level is not None:
            place = MAIN * room + jnp.where(me == 0, 0, room - 1 - n)
        else:
            place = slot // slots * room + slots + slot % slots
        far = arrived_ref[pl.ds(place, 1), :]
        lands = jnp.where(me == 0, jnp.minimum(table_ref[Table.PARTNER * nb + slot], rows - 1), 0)
        near = matrix_ref[pl.ds(lands, 1), :]
        out_ref[pl.ds(table_ref[Table.ROW * nb + slot] - me * rows, 1), :] = jnp.where(me == 0, near, far)
        return 0

    lax.fori_loop(0, table_ref[Table.COUNT * nb], patch, 0)
    upper = upper_ref[...].reshape(nb, cols)
    top = dot(inverse_ref[:half], upper[:half])
    rest = upper[half:] - dot(lower_ref[...], top)
    upper = jnp.concatenate([top, dot(inverse_ref[half:], rest)], axis=0)
    out_ref[...] -= dot(panel_ref[...], upper)

    @pl.when(me == 0)
    def _():
        out_ref[:nb, :] = upper


def call(kernel, outs, in_specs, out_specs, scratch=()):
    return pl.pallas_call(
        kernel,
        out_shape=outs,
        in_specs=in_specs,
        out_specs=out_specs,
        scratch_shapes=list(scratch),
        compiler_params=pltpu.CompilerParams(vmem_limit_bytes=16 * 1024 * 1024),
    )


def exchange(value, place):
    planes = value.shape[0]
    order = [[(p - place) % planes for p in range(planes)]]
    return lax.all_to_all(value, "prow", 0, 0, axis_index_groups=order)


def local(matrix, factored_panel, pivots):
    rows, cols = matrix.shape
    nb = pivots.shape[0]
    planes = lax.axis_size("prow")
    slots = nb // planes
    width = factored_panel.shape[1]
    rooms = ROUNDS
    f32 = jnp.float32
    panel = factored_panel.T
    pieces = call(spread_kernel, jax.ShapeDtypeStruct((planes, width, nb), f32), [VMEM], VMEM)(panel)
    pieces = exchange(pieces, EARLY)
    *sends, level, table = call(
        pack_kernel,
        (
            *(jax.ShapeDtypeStruct((planes * room, cols), f32) for room in rooms),
            jax.ShapeDtypeStruct((1,), jnp.int32),
            jax.ShapeDtypeStruct((8 * nb,), jnp.int32),
        ),
        [SMEM, HBM],
        (*(VMEM for _ in rooms), SMEM, SMEM),
        [
            pltpu.SMEM((rows * planes,), jnp.int32),
            pltpu.SMEM((len(rooms) * planes,), jnp.int32),
            pltpu.VMEM((rows, cols), f32),
            pltpu.SemaphoreType.DMA,
        ],
    )(pivots, matrix)

    def finish(level, table, panel, pieces, arrived, matrix):
        pieces = call(join_kernel, jax.ShapeDtypeStruct((width, rows + nb), f32), [VMEM, VMEM], VMEM)(panel, pieces)
        gathered = lax.all_gather(pieces, "pcol", axis=0, tiled=True)
        by_rows = call(
            invert_kernel,
            (
                jax.ShapeDtypeStruct((rows, nb), f32),
                jax.ShapeDtypeStruct((nb, nb // 2), f32),
                jax.ShapeDtypeStruct((nb // 2, nb // 2), f32),
            ),
            [VMEM],
            (VMEM, VMEM, VMEM),
        )(gathered)
        return call(
            partial(update_kernel, level),
            jax.ShapeDtypeStruct((rows, cols), f32),
            [SMEM, VMEM, VMEM, VMEM, VMEM, VMEM],
            VMEM,
            [pltpu.VMEM((planes, slots, cols), f32)],
        )(table, *by_rows, arrived, matrix)

    def one_round(level, sends, table, panel, pieces, matrix):
        arrived = exchange(sends[level].reshape(planes, rooms[level], cols), MAIN)
        return finish(level, table, panel, pieces, arrived.reshape(planes * rooms[level], cols), matrix)

    def two_rounds(sends, table, panel, pieces, matrix):
        slot = jax.ShapeDtypeStruct((planes, slots, cols), f32)
        both = jax.ShapeDtypeStruct((planes, 2 * slots, cols), f32)
        arrived = exchange(call(slot_kernel, slot, [SMEM, VMEM], VMEM)(table, matrix), 0)
        send = call(partial(sort_kernel, rows), both, [SMEM, VMEM], VMEM)(table, arrived)
        arrived = exchange(send, 0)
        return finish(None, table, panel, pieces, arrived.reshape(2 * nb, cols), matrix)

    forms = [*(partial(one_round, level) for level in range(len(rooms))), two_rounds]
    return lax.switch(level[0], forms, sends, table, panel, pieces, matrix)


def solution(mesh):
    return jax.shard_map(
        local,
        mesh=mesh,
        in_specs=(P("prow", "pcol"), P("prow", "pcol"), P()),
        out_specs=P("prow", "pcol"),
        check_vma=False,
    )
```

```python
from functools import partial

import jax
import jax.numpy as jnp
from jax import lax
from jax.experimental import pallas as pl
from jax.experimental.pallas import tpu as pltpu
from jax.sharding import PartitionSpec as P

HIGHEST = lax.Precision.HIGHEST
ROUNDS = (40, 48)
EARLY = 4
MAIN = 4
VMEM = pl.BlockSpec(memory_space=pltpu.VMEM)
HBM = pl.BlockSpec(memory_space=pltpu.HBM)
SMEM = pl.BlockSpec(memory_space=pltpu.SMEM)


def dot(a, b):
    return jnp.dot(a, b, precision=HIGHEST, preferred_element_type=jnp.float32)


class Table:
    ROW, PARTNER, OWN, COUNT, PLACE = range(5)


def spread_kernel(panel_ref, send_ref):
    nb = send_ref.shape[2]
    piece = panel_ref[:, :nb]
    for d in range(send_ref.shape[0]):
        send_ref[d] = piece


def join_kernel(panel_ref, pieces_ref, out_ref):
    rows = panel_ref.shape[1]
    out_ref[:, :rows] = panel_ref[...]
    out_ref[:, rows:] = pieces_ref[EARLY % pieces_ref.shape[0]]


def pack_kernel(pivots_ref, matrix_hbm, *refs):
    *send_refs, level_ref, table_ref, order_ref, fill_ref, matrix_ref, sem = refs
    nb = pivots_ref.shape[0]
    rows = matrix_ref.shape[0]
    planes = fill_ref.shape[0] // len(send_refs)
    rooms = [send_ref.shape[0] // planes for send_ref in send_refs]
    me = lax.axis_index("prow")
    bits = rows.bit_length() - 1
    fetch_matrix = pltpu.make_async_copy(matrix_hbm, matrix_ref, sem)
    fetch_matrix.start()

    def start(j, _):
        target = pivots_ref[j]
        order_ref[target] = target
        order_ref[j] = j
        return 0

    lax.fori_loop(0, nb, start, 0, unroll=16)

    def first_place(plane, room):
        return ((plane + MAIN) & (planes - 1)) * room

    for d in range(planes):
        for n, room in enumerate(rooms):
            fill_ref[n * planes + d] = first_place(d, room)

    mine_from = first_place(me, rooms[0])

    def exchange(j, _):
        target = pivots_ref[j]
        first = order_ref[j]
        row = order_ref[target]
        order_ref[target] = first
        table_ref[Table.ROW * nb + j] = row
        owner = row >> bits
        for n in range(len(rooms)):
            place = fill_ref[n * planes + owner]
            fill_ref[n * planes + owner] = place + 1
            table_ref[(Table.PLACE + n) * nb + j] = place
            if n == 0:
                own = Table.OWN * nb - mine_from + place
        table_ref[jnp.where(owner == me, own, Table.COUNT * nb)] = j
        return 0

    lax.fori_loop(0, nb, exchange, 0, unroll=16)
    count = fill_ref[me] - mine_from
    table_ref[Table.COUNT * nb] = count
    most = 0
    for d in range(1, planes):
        most = jnp.maximum(most, fill_ref[d] - first_place(d, rooms[0]))

    most = fill_ref[0] - first_place(0, rooms[0]) + most
    level = len(rooms)
    for n in reversed(range(len(rooms))):
        level = jnp.where(most <= rooms[n], n, level)
    level_ref[0] = level

    @pl.when((me == 0) & (level == len(rooms)))
    def _():
        def meet(i, _):
            table_ref[Table.PARTNER * nb + i] = order_ref[table_ref[Table.ROW * nb + i]]
            return 0

        lax.fori_loop(0, nb, meet, 0, unroll=16)

    fetch_matrix.wait()

    def fill(n, send_ref, room):
        def give(k, _):
            slot = table_ref[Table.OWN * nb + k]
            row = table_ref[Table.ROW * nb + slot]
            table_ref[Table.PARTNER * nb + slot] = order_ref[row]
            mine = row & (rows - 1)
            send_ref[pl.ds(k, 1), :] = matrix_ref[pl.ds(mine, 1), :]
            return 0

        lax.fori_loop(0, count, give, 0)
        given = send_ref[:room, :]
        for d in range(1, planes):
            send_ref[d * room : (d + 1) * room, :] = given

        @pl.when(me == 0)
        def _():
            def hand(i, _):
                row = table_ref[Table.ROW * nb + i]
                away = row >= rows
                partner = jnp.where(away, order_ref[row], 0)
                put = 2 * first_place(row >> bits, room) + room - 1 - table_ref[(Table.PLACE + n) * nb + i]
                put = jnp.where(away, put, (MAIN + 1) * room - 1)
                send_ref[pl.ds(put, 1), :] = matrix_ref[pl.ds(partner, 1), :]
                return 0

            lax.fori_loop(0, nb, hand, 0, unroll=16)

    for n, send_ref in enumerate(send_refs):
        pl.when(level == n)(partial(fill, n, send_ref, rooms[n]))


def slot_kernel(table_ref, matrix_ref, send_ref):
    planes, slots, _ = send_ref.shape
    nb = planes * slots
    rows = matrix_ref.shape[0]
    me = lax.axis_index("prow")

    def place(d, _):
        for k in range(slots):
            i = d * slots + k
            mine = table_ref[Table.ROW * nb + i] - me * rows
            owned = (mine >= 0) & (mine < rows)
            take = jnp.where(owned, mine, jnp.where(me == 0, table_ref[Table.PARTNER * nb + i], 0))
            send_ref[d, k : k + 1, :] = matrix_ref[pl.ds(take, 1), :]
        return 0

    lax.fori_loop(0, planes, place, 0)


def sort_kernel(rows, table_ref, arrived_ref, send_ref):
    planes, slots, _ = arrived_ref.shape
    me = lax.axis_index("prow")
    for k in range(slots):
        owner = table_ref[me * slots + k] // rows
        send_ref[0, k : k + 1, :] = arrived_ref[owner, k : k + 1, :]
    send_ref[0, slots:, :] = arrived_ref[0]
    both = send_ref[0]
    for d in range(1, planes):
        send_ref[d] = both


def invert_upper(block):
    size = block.shape[0]
    row = lax.broadcasted_iota(jnp.int32, (size, size), 0)
    col = lax.broadcasted_iota(jnp.int32, (size, size), 1)
    inverse = None
    width = 1
    while width < size:
        pair = ((row ^ col) & ~(2 * width - 1)) == 0
        cross = jnp.where(pair & ((row & width) == 0) & ((col & width) != 0), block, 0.0)
        if inverse is None:
            inverse = jnp.where(row == col, 1.0, 0.0) - cross
        else:
            inverse = inverse - dot(dot(inverse, cross), inverse)
        width *= 2
    return inverse


def invert_kernel(gathered_ref, panel_ref, inverse_ref, lower_ref):
    rows, nb = panel_ref.shape
    half = nb // 2
    inverse_ref[:half] = invert_upper(gathered_ref[:half, rows : rows + half]).T
    inverse_ref[half:] = invert_upper(gathered_ref[half:, rows + half :]).T
    lower_ref[...] = gathered_ref[:half, rows + half :].T
    panel_ref[...] = gathered_ref[:, :rows].T


def update_kernel(level, table_ref, panel_ref, inverse_ref, lower_ref, arrived_ref, matrix_ref, out_ref, upper_ref):
    planes, slots, cols = upper_ref.shape
    nb = planes * slots
    rows = matrix_ref.shape[0]
    room = arrived_ref.shape[0] // planes
    half = nb // 2
    me = lax.axis_index("prow")

    for d in range(planes):
        for k in range(slots):
            place = d * room + k
            if level is not None:
                place = table_ref[(Table.PLACE + level) * nb + d * slots + k]
            upper_ref[d, k : k + 1, :] = arrived_ref[pl.ds(place, 1), :]
    out_ref[...] = matrix_ref[...]

    def patch(n, _):
        slot = table_ref[Table.OWN * nb + n]
        if level is not None:
            place = MAIN * room + jnp.where(me == 0, 0, room - 1 - n)
        else:
            place = slot // slots * room + slots + slot % slots
        far = arrived_ref[pl.ds(place, 1), :]
        lands = jnp.where(me == 0, jnp.minimum(table_ref[Table.PARTNER * nb + slot], rows - 1), 0)
        near = matrix_ref[pl.ds(lands, 1), :]
        out_ref[pl.ds(table_ref[Table.ROW * nb + slot] - me * rows, 1), :] = jnp.where(me == 0, near, far)
        return 0

    lax.fori_loop(0, table_ref[Table.COUNT * nb], patch, 0)
    upper = upper_ref[...].reshape(nb, cols)
    top = dot(inverse_ref[:half], upper[:half])
    rest = upper[half:] - dot(lower_ref[...], top)
    upper = jnp.concatenate([top, dot(inverse_ref[half:], rest)], axis=0)
    out_ref[...] -= dot(panel_ref[...], upper)

    @pl.when(me == 0)
    def _():
        out_ref[:nb, :] = upper


def call(kernel, outs, in_specs, out_specs, scratch=()):
    return pl.pallas_call(
        kernel,
        out_shape=outs,
        in_specs=in_specs,
        out_specs=out_specs,
        scratch_shapes=list(scratch),
        compiler_params=pltpu.CompilerParams(vmem_limit_bytes=16 * 1024 * 1024),
    )


def exchange(value, place):
    planes = value.shape[0]
    order = [[(p - place) % planes for p in range(planes)]]
    return lax.all_to_all(value, "prow", 0, 0, axis_index_groups=order)


def local(matrix, factored_panel, pivots):
    rows, cols = matrix.shape
    nb = pivots.shape[0]
    planes = lax.axis_size("prow")
    slots = nb // planes
    width = factored_panel.shape[1]
    rooms = ROUNDS
    f32 = jnp.float32
    panel = factored_panel.T
    pieces = call(spread_kernel, jax.ShapeDtypeStruct((planes, width, nb), f32), [VMEM], VMEM)(panel)
    pieces = exchange(pieces, EARLY)
    *sends, level, table = call(
        pack_kernel,
        (
            *(jax.ShapeDtypeStruct((planes * room, cols), f32) for room in rooms),
            jax.ShapeDtypeStruct((1,), jnp.int32),
            jax.ShapeDtypeStruct((8 * nb,), jnp.int32),
        ),
        [SMEM, HBM],
        (*(VMEM for _ in rooms), SMEM, SMEM),
        [
            pltpu.SMEM((rows * planes,), jnp.int32),
            pltpu.SMEM((len(rooms) * planes,), jnp.int32),
            pltpu.VMEM((rows, cols), f32),
            pltpu.SemaphoreType.DMA,
        ],
    )(pivots, matrix)

    def finish(level, table, panel, pieces, arrived, matrix):
        pieces = call(join_kernel, jax.ShapeDtypeStruct((width, rows + nb), f32), [VMEM, VMEM], VMEM)(panel, pieces)
        gathered = lax.all_gather(pieces, "pcol", axis=0, tiled=True)
        by_rows = call(
            invert_kernel,
            (
                jax.ShapeDtypeStruct((rows, nb), f32),
                jax.ShapeDtypeStruct((nb, nb // 2), f32),
                jax.ShapeDtypeStruct((nb // 2, nb // 2), f32),
            ),
            [VMEM],
            (VMEM, VMEM, VMEM),
        )(gathered)
        return call(
            partial(update_kernel, level),
            jax.ShapeDtypeStruct((rows, cols), f32),
            [SMEM, VMEM, VMEM, VMEM, VMEM, VMEM],
            VMEM,
            [pltpu.VMEM((planes, slots, cols), f32)],
        )(table, *by_rows, arrived, matrix)

    def one_round(level, sends, table, panel, pieces, matrix):
        arrived = exchange(sends[level].reshape(planes, rooms[level], cols), MAIN)
        return finish(level, table, panel, pieces, arrived.reshape(planes * rooms[level], cols), matrix)

    def two_rounds(sends, table, panel, pieces, matrix):
        slot = jax.ShapeDtypeStruct((planes, slots, cols), f32)
        both = jax.ShapeDtypeStruct((planes, 2 * slots, cols), f32)
        arrived = exchange(call(slot_kernel, slot, [SMEM, VMEM], VMEM)(table, matrix), 0)
        send = call(partial(sort_kernel, rows), both, [SMEM, VMEM], VMEM)(table, arrived)
        arrived = exchange(send, 0)
        return finish(None, table, panel, pieces, arrived.reshape(2 * nb, cols), matrix)

    forms = [*(partial(one_round, level) for level in range(len(rooms))), two_rounds]
    return lax.switch(level[0], forms, sends, table, panel, pieces, matrix)


def solution(mesh):
    return jax.shard_map(
        local,
        mesh=mesh,
        in_specs=(P("prow", "pcol"), P("prow", "pcol"), P()),
        out_specs=P("prow", "pcol"),
        check_vma=False,
    )
```

```python
from functools import partial

import jax
import jax.numpy as jnp
from jax import lax
from jax.experimental import pallas as pl
from jax.experimental.pallas import tpu as pltpu
from jax.sharding import PartitionSpec as P

HIGHEST = lax.Precision.HIGHEST
ROUNDS = (40, 48)
EARLY = 4
MAIN = 4
VMEM = pl.BlockSpec(memory_space=pltpu.VMEM)
HBM = pl.BlockSpec(memory_space=pltpu.HBM)
SMEM = pl.BlockSpec(memory_space=pltpu.SMEM)


def dot(a, b):
    return jnp.dot(a, b, precision=HIGHEST, preferred_element_type=jnp.float32)


class Table:
    ROW, PARTNER, OWN, COUNT, PLACE = range(5)


def spread_kernel(panel_ref, send_ref):
    nb = send_ref.shape[2]
    piece = panel_ref[:, :nb]
    for d in range(send_ref.shape[0]):
        send_ref[d] = piece


def join_kernel(panel_ref, pieces_ref, out_ref):
    rows = panel_ref.shape[1]
    out_ref[:, :rows] = panel_ref[...]
    out_ref[:, rows:] = pieces_ref[EARLY % pieces_ref.shape[0]]


def pack_kernel(pivots_ref, matrix_hbm, *refs):
    *send_refs, level_ref, table_ref, order_ref, fill_ref, matrix_ref, sem = refs
    nb = pivots_ref.shape[0]
    rows = matrix_ref.shape[0]
    planes = fill_ref.shape[0] // len(send_refs)
    rooms = [send_ref.shape[0] // planes for send_ref in send_refs]
    me = lax.axis_index("prow")
    bits = rows.bit_length() - 1
    fetch_matrix = pltpu.make_async_copy(matrix_hbm, matrix_ref, sem)
    fetch_matrix.start()

    def start(j, _):
        target = pivots_ref[j]
        order_ref[target] = target
        order_ref[j] = j
        return 0

    lax.fori_loop(0, nb, start, 0, unroll=16)

    def first_place(plane, room):
        return ((plane + MAIN) & (planes - 1)) * room

    for d in range(planes):
        for n, room in enumerate(rooms):
            fill_ref[n * planes + d] = first_place(d, room)

    mine_from = first_place(me, rooms[0])

    def exchange(j, _):
        target = pivots_ref[j]
        first = order_ref[j]
        row = order_ref[target]
        order_ref[target] = first
        table_ref[Table.ROW * nb + j] = row
        owner = row >> bits
        for n in range(len(rooms)):
            place = fill_ref[n * planes + owner]
            fill_ref[n * planes + owner] = place + 1
            table_ref[(Table.PLACE + n) * nb + j] = place
            if n == 0:
                own = Table.OWN * nb - mine_from + place
        table_ref[jnp.where(owner == me, own, Table.COUNT * nb)] = j
        return 0

    lax.fori_loop(0, nb, exchange, 0, unroll=16)
    count = fill_ref[me] - mine_from
    table_ref[Table.COUNT * nb] = count
    most = 0
    for d in range(1, planes):
        most = jnp.maximum(most, fill_ref[d] - first_place(d, rooms[0]))

    most = fill_ref[0] - first_place(0, rooms[0]) + most
    level = len(rooms)
    for n in reversed(range(len(rooms))):
        level = jnp.where(most <= rooms[n], n, level)
    level_ref[0] = level

    @pl.when((me == 0) & (level == len(rooms)))
    def _():
        def meet(i, _):
            table_ref[Table.PARTNER * nb + i] = order_ref[table_ref[Table.ROW * nb + i]]
            return 0

        lax.fori_loop(0, nb, meet, 0, unroll=16)

    fetch_matrix.wait()

    def fill(n, send_ref, room):
        def give(k, _):
            slot = table_ref[Table.OWN * nb + k]
            row = table_ref[Table.ROW * nb + slot]
            table_ref[Table.PARTNER * nb + slot] = order_ref[row]
            mine = row & (rows - 1)
            send_ref[pl.ds(k, 1), :] = matrix_ref[pl.ds(mine, 1), :]
            return 0

        lax.fori_loop(0, count, give, 0)
        given = send_ref[:room, :]
        for d in range(1, planes):
            send_ref[d * room : (d + 1) * room, :] = given

        @pl.when(me == 0)
        def _():
            def hand(i, _):
                row = table_ref[Table.ROW * nb + i]
                away = row >= rows
                partner = jnp.where(away, order_ref[row], 0)
                put = 2 * first_place(row >> bits, room) + room - 1 - table_ref[(Table.PLACE + n) * nb + i]
                put = jnp.where(away, put, (MAIN + 1) * room - 1)
                send_ref[pl.ds(put, 1), :] = matrix_ref[pl.ds(partner, 1), :]
                return 0

            lax.fori_loop(0, nb, hand, 0, unroll=16)

    for n, send_ref in enumerate(send_refs):
        pl.when(level == n)(partial(fill, n, send_ref, rooms[n]))


def slot_kernel(table_ref, matrix_ref, send_ref):
    planes, slots, _ = send_ref.shape
    nb = planes * slots
    rows = matrix_ref.shape[0]
    me = lax.axis_index("prow")

    def place(d, _):
        for k in range(slots):
            i = d * slots + k
            mine = table_ref[Table.ROW * nb + i] - me * rows
            owned = (mine >= 0) & (mine < rows)
            take = jnp.where(owned, mine, jnp.where(me == 0, table_ref[Table.PARTNER * nb + i], 0))
            send_ref[d, k : k + 1, :] = matrix_ref[pl.ds(take, 1), :]
        return 0

    lax.fori_loop(0, planes, place, 0)


def sort_kernel(rows, table_ref, arrived_ref, send_ref):
    planes, slots, _ = arrived_ref.shape
    me = lax.axis_index("prow")
    for k in range(slots):
        owner = table_ref[me * slots + k] // rows
        send_ref[0, k : k + 1, :] = arrived_ref[owner, k : k + 1, :]
    send_ref[0, slots:, :] = arrived_ref[0]
    both = send_ref[0]
    for d in range(1, planes):
        send_ref[d] = both


def invert_upper(block):
    size = block.shape[0]
    row = lax.broadcasted_iota(jnp.int32, (size, size), 0)
    col = lax.broadcasted_iota(jnp.int32, (size, size), 1)

    def cross(width):
        pair = ((row ^ col) & ~(2 * width - 1)) == 0
        return jnp.where(pair & ((row & width) == 0) & ((col & width) != 0), block, 0.0)

    inverse = jnp.where(row == col, 1.0, 0.0) - cross(1)
    width = 2
    while width < size:
        near = dot(inverse, cross(width))
        if 2 * width < size:
            far = dot(inverse, cross(2 * width))
            far = far - dot(near, far)
        inverse = inverse - dot(near, inverse)
        if 2 * width < size:
            inverse = inverse - dot(far, inverse)
        width *= 4
    return inverse


def invert_kernel(gathered_ref, panel_ref, inverse_ref, lower_ref):
    rows, nb = panel_ref.shape
    half = nb // 2
    inverse_ref[:half] = invert_upper(gathered_ref[:half, rows : rows + half]).T
    inverse_ref[half:] = invert_upper(gathered_ref[half:, rows + half :]).T
    lower_ref[...] = gathered_ref[:half, rows + half :].T
    panel_ref[...] = gathered_ref[:, :rows].T


def update_kernel(level, table_ref, panel_ref, inverse_ref, lower_ref, arrived_ref, matrix_ref, out_ref, upper_ref):
    planes, slots, cols = upper_ref.shape
    nb = planes * slots
    rows = matrix_ref.shape[0]
    room = arrived_ref.shape[0] // planes
    half = nb // 2
    me = lax.axis_index("prow")

    for d in range(planes):
        for k in range(slots):
            place = d * room + k
            if level is not None:
                place = table_ref[(Table.PLACE + level) * nb + d * slots + k]
            upper_ref[d, k : k + 1, :] = arrived_ref[pl.ds(place, 1), :]
    out_ref[...] = matrix_ref[...]

    def patch(n, _):
        slot = table_ref[Table.OWN * nb + n]
        if level is not None:
            place = MAIN * room + jnp.where(me == 0, 0, room - 1 - n)
        else:
            place = slot // slots * room + slots + slot % slots
        far = arrived_ref[pl.ds(place, 1), :]
        lands = jnp.where(me == 0, jnp.minimum(table_ref[Table.PARTNER * nb + slot], rows - 1), 0)
        near = matrix_ref[pl.ds(lands, 1), :]
        out_ref[pl.ds(table_ref[Table.ROW * nb + slot] - me * rows, 1), :] = jnp.where(me == 0, near, far)
        return 0

    lax.fori_loop(0, table_ref[Table.COUNT * nb], patch, 0)
    upper = upper_ref[...].reshape(nb, cols)
    top = dot(inverse_ref[:half], upper[:half])
    rest = upper[half:] - dot(lower_ref[...], top)
    upper = jnp.concatenate([top, dot(inverse_ref[half:], rest)], axis=0)
    out_ref[...] -= dot(panel_ref[...], upper)

    @pl.when(me == 0)
    def _():
        out_ref[:nb, :] = upper


def call(kernel, outs, in_specs, out_specs, scratch=()):
    return pl.pallas_call(
        kernel,
        out_shape=outs,
        in_specs=in_specs,
        out_specs=out_specs,
        scratch_shapes=list(scratch),
        compiler_params=pltpu.CompilerParams(vmem_limit_bytes=16 * 1024 * 1024),
    )


def exchange(value, place):
    planes = value.shape[0]
    order = [[(p - place) % planes for p in range(planes)]]
    return lax.all_to_all(value, "prow", 0, 0, axis_index_groups=order)


def local(matrix, factored_panel, pivots):
    rows, cols = matrix.shape
    nb = pivots.shape[0]
    planes = lax.axis_size("prow")
    slots = nb // planes
    width = factored_panel.shape[1]
    rooms = ROUNDS
    f32 = jnp.float32
    panel = factored_panel.T
    pieces = call(spread_kernel, jax.ShapeDtypeStruct((planes, width, nb), f32), [VMEM], VMEM)(panel)
    pieces = exchange(pieces, EARLY)
    *sends, level, table = call(
        pack_kernel,
        (
            *(jax.ShapeDtypeStruct((planes * room, cols), f32) for room in rooms),
            jax.ShapeDtypeStruct((1,), jnp.int32),
            jax.ShapeDtypeStruct((8 * nb,), jnp.int32),
        ),
        [SMEM, HBM],
        (*(VMEM for _ in rooms), SMEM, SMEM),
        [
            pltpu.SMEM((rows * planes,), jnp.int32),
            pltpu.SMEM((len(rooms) * planes,), jnp.int32),
            pltpu.VMEM((rows, cols), f32),
            pltpu.SemaphoreType.DMA,
        ],
    )(pivots, matrix)

    def finish(level, table, panel, pieces, arrived, matrix):
        pieces = call(join_kernel, jax.ShapeDtypeStruct((width, rows + nb), f32), [VMEM, VMEM], VMEM)(panel, pieces)
        gathered = lax.all_gather(pieces, "pcol", axis=0, tiled=True)
        by_rows = call(
            invert_kernel,
            (
                jax.ShapeDtypeStruct((rows, nb), f32),
                jax.ShapeDtypeStruct((nb, nb // 2), f32),
                jax.ShapeDtypeStruct((nb // 2, nb // 2), f32),
            ),
            [VMEM],
            (VMEM, VMEM, VMEM),
        )(gathered)
        return call(
            partial(update_kernel, level),
            jax.ShapeDtypeStruct((rows, cols), f32),
            [SMEM, VMEM, VMEM, VMEM, VMEM, VMEM],
            VMEM,
            [pltpu.VMEM((planes, slots, cols), f32)],
        )(table, *by_rows, arrived, matrix)

    def one_round(level, sends, table, panel, pieces, matrix):
        arrived = exchange(sends[level].reshape(planes, rooms[level], cols), MAIN)
        return finish(level, table, panel, pieces, arrived.reshape(planes * rooms[level], cols), matrix)

    def two_rounds(sends, table, panel, pieces, matrix):
        slot = jax.ShapeDtypeStruct((planes, slots, cols), f32)
        both = jax.ShapeDtypeStruct((planes, 2 * slots, cols), f32)
        arrived = exchange(call(slot_kernel, slot, [SMEM, VMEM], VMEM)(table, matrix), 0)
        send = call(partial(sort_kernel, rows), both, [SMEM, VMEM], VMEM)(table, arrived)
        arrived = exchange(send, 0)
        return finish(None, table, panel, pieces, arrived.reshape(2 * nb, cols), matrix)

    forms = [*(partial(one_round, level) for level in range(len(rooms))), two_rounds]
    return lax.switch(level[0], forms, sends, table, panel, pieces, matrix)


def solution(mesh):
    return jax.shard_map(
        local,
        mesh=mesh,
        in_specs=(P("prow", "pcol"), P("prow", "pcol"), P()),
        out_specs=P("prow", "pcol"),
        check_vma=False,
    )
```
